32 devices in a mesh: group: 2 (over y), expert: 8 (over z, x), tensor: 2 (over core).
Axes of the slice: x: 2, y: 2, z: 4, core: 2. Of those that a mesh axis runs over, the one named last changes fastest.
Arguments:
- tokens: bfloat16 [1024, 3072], P(('group', 'expert'), 'tensor'), parts along dimension 0, may hold values from -6 to 6
- route_ids: int32 [1024, 4], P(('group', 'expert')), parts along dimension 0, may hold values from 0 to 7, all different within a row; in each aligned block of 64 rows (0 to 63, 64 to 127, ...) at most 64 rows name the same one
- gates: float32 [1024, 4], P(('group', 'expert')), parts along dimension 0, may hold values from 0.1 to 1
- w_up: bfloat16 [8, 3072, 5376], P('expert', None, 'tensor'), may hold values from -0.109375 to 0.109375
- w_down: bfloat16 [8, 5376, 3072], P('expert', 'tensor'), may hold values from -0.109375 to 0.109375
Outputs:
- mixed: bfloat16 [1024, 3072], P(('group', 'expert'), 'tensor'), parts along dimension 0
The draws below stay inside these ranges and needn't reach their ends.
There are 2 independent parts, one for each index of `group`. The reference program is written for one: setup_inputs(seed, part) draws one part's arguments, and reference() takes and returns one part's arrays. A program takes and returns all parts, laid end to end along the dimension named above; an argument that names none is the same for every part. Nothing has to cross between parts.
Inputs may be any that keep to these rules, and one draw needn't show every extreme that they name: `route_ids`: among the 64 rows of one owner, no expert is named by more than 64 routes, and in every draw some expert is named by exactly 64; each row names 4 different experts.
All inputs are finite; a program needn't handle non-finite values.
Results may differ from the reference program's by a relative error of at most 0.0085.
Values may be sent and summed in bfloat16 or wider, within the bound.
A program may use at most 128 MiB of HBM per device.

```python
import math
import jax
import jax.numpy as jnp
import numpy as np
from jax import lax

D = 3072
FF = 5376
TOP = 4
TOK_DEV = 64
EXPERTS = 8
CAP = 64
TOKENS = 512
N_EXPERT = 8
N_TENSOR = 2


def spiked(drawn, stream_key, source, target, parts, factor):
    def block_of(dim):
        return (jnp.arange(drawn.shape[dim]) // (drawn.shape[dim] // parts)).reshape((-1,) + (1,) * (drawn.ndim - 1 - dim))

    near = jax.random.permutation(stream_key, parts)[block_of(target)]
    other_side = (block_of(target) + parts // 2) % parts
    return jnp.where((block_of(source) == near) | (block_of(source) == other_side), factor * drawn, drawn)


def block_levels(stream_key, extent, cuts, smallest, top_value):
    gain, own = 1.0, jax.random.fold_in(stream_key, 6)
    for dim, parts in cuts:
        heights = jnp.exp(jax.random.uniform(jax.random.fold_in(own, dim), (parts,), jnp.float32, smallest / len(cuts), top_value / len(cuts)))
        gain = gain * jnp.repeat(heights, extent[dim] // parts).reshape([-1 if axis == dim else 1 for axis in range(len(extent))])
    return gain


def routed_block(stream_key, own, number, rows, amount, top, reach, lean):
    ranking = jax.random.permutation(stream_key, amount)
    heavy_load, ordinary = shares(amount, rows * top, reach, lean, True), shares(amount, rows * top, reach, lean, False)
    places = jnp.arange(amount)

    def named(sizes, offset_by):
        used = int((sizes > 0).sum())
        fixed = max(1, used // 4)
        shifted = fixed + (places - fixed + offset_by * (used - fixed)) % max(1, amount - fixed)
        return jnp.zeros((amount,), jnp.int32).at[ranking[jnp.where(places < fixed, places, shifted)]].set(jnp.asarray(sizes, jnp.int32))

    sizes = jnp.where(number % 4 == 0, named(heavy_load, number // 4), named(ordinary, number - number // 4 - 1))
    mixed = jax.random.permutation(jax.random.fold_in(own, 3), amount)
    source_of, taker = mixed[0:amount // 2 * 2:2], mixed[1:amount // 2 * 2:2]
    margin = jnp.minimum(sizes[source_of] - 1, reach - sizes[taker]) // 2
    margin = jnp.where((source_of == ranking[0]) | (taker == ranking[0]) | (sizes[taker] == 0), 0, jnp.maximum(margin, 0))
    shifted = jax.random.randint(jax.random.fold_in(own, 4), (amount // 2,), 0, 1 << 20) % (margin + 1)
    sizes = sizes.at[source_of].add(-shifted).at[taker].add(shifted)
    items = jnp.searchsorted(jnp.cumsum(sizes), jnp.arange(rows * top), side="right").astype(jnp.int32)
    table = items.reshape(top, rows).T
    table = table[jax.random.permutation(jax.random.fold_in(own, 1), rows)]
    offset_by = jax.random.randint(jax.random.fold_in(own, 2), (rows, 1), 0, top)
    return jnp.take_along_axis(table, (jnp.arange(top)[None, :] + offset_by) % top, axis=1)


def shares(number_of, total, reach, slope, full):
    weights = [(1 << 20) // math.isqrt(grade ** slope) + 1 for grade in range(1, number_of + 1)]
    largest = reach if full else min(reach, max(-(-total // number_of), total * weights[0] // sum(weights)))
    least = 1 if total - largest >= number_of - 1 else 0
    given, surplus = [largest] + [least] * (number_of - 1), total - largest - least * (number_of - 1)
    while surplus > 0:
        free = [i for i in range(1, number_of) if given[i] < largest] or [i for i in range(1, number_of) if given[i] < reach]
        whole, remaining = sum([weights[i] for i in free]), surplus
        for i in free:
            addition = min(reach - given[i], max(1, remaining * weights[i] // whole), surplus)
            given[i] = given[i] + addition
            surplus = surplus - addition
    return np.array(given)


def noise(stream_key, extent, deviation, reach, split=(), kind=jnp.bfloat16):
    loudness = block_levels(stream_key, extent, split, -0.22, 0.18) if split else 1.0
    result = jax.random.normal(stream_key, extent, jnp.float32) * deviation * loudness
    return jnp.minimum(jnp.maximum(result, -reach), reach).astype(kind)


def gaussian_with(rng, dims, width, bound, split, heavy, kind=jnp.bfloat16):
    array = width * jax.random.normal(rng, dims, jnp.float32)
    if split:
        array = array * block_levels(rng, dims, split, -0.22, 0.18)
    return jnp.clip(spiked(array, jax.random.fold_in(rng, 3), *heavy), -bound, bound).astype(kind)


def setup_inputs(seed: int = 0, part: int = 0) -> dict:
    keys = jax.random.split(jax.random.key(seed), 6)
    part_keys = jax.random.split(jax.random.fold_in(keys[5], part), 6)
    tokens = noise(part_keys[0], (TOKENS, D), 1.0, 6.0, ((0, 8), (1, 2)))
    route_ids_keys = jax.random.split(jax.random.fold_in(part_keys[1], 1), TOKENS // TOK_DEV)
    route_ids_turns = jax.random.permutation(jax.random.fold_in(part_keys[1], 3), TOKENS // TOK_DEV)
    route_ids = jax.vmap(lambda own, number: routed_block(jax.random.fold_in(part_keys[1], 2), own, number, TOK_DEV, EXPERTS, TOP, CAP, 2))(route_ids_keys, route_ids_turns).reshape((TOKENS, TOP))
    gates = jnp.clip(jnp.exp(math.log(1.0) - 2.3025851 * jax.random.uniform(part_keys[2], (TOKENS, TOP), jnp.float32) ** block_levels(part_keys[2], (TOKENS, TOP), ((0, 8),), -0.2, 0.2)), 0.1, 1.0)
    w_up = noise(keys[3], (EXPERTS, D, FF), D ** -0.5, 0.109375, ((0, 8), (2, 2)))
    w_down = gaussian_with(keys[4], (EXPERTS, FF, D), FF ** -0.5, 0.109375, ((0, 8), (1, 2)), (1, 2, 2, 2.0))
    return dict(tokens=tokens, route_ids=route_ids, gates=gates, w_up=w_up, w_down=w_down)


def reference(tokens, route_ids, gates, w_up, w_down):
    owner_ids = route_ids.reshape(N_EXPERT, TOK_DEV * TOP)
    onehot = (owner_ids[:, :, None] == jnp.arange(EXPERTS, dtype=jnp.int32)[None, None, :]).astype(jnp.int32)
    within = jnp.sum((jnp.cumsum(onehot, axis=1) - onehot) * onehot, axis=2)
    sources = jnp.arange(N_EXPERT, dtype=jnp.int32)[:, None]
    position = (sources * CAP + within).reshape(-1).astype(jnp.int32)
    route_order = jnp.arange(TOK_DEV * TOP, dtype=jnp.int32)[None, :] // TOP
    owner_token = (sources * TOK_DEV + route_order).reshape(-1).astype(jnp.int32)
    expert_ids = route_ids.reshape(-1).astype(jnp.int32)
    table = jnp.zeros((EXPERTS, N_EXPERT * CAP), jnp.int32).at[expert_ids, position].set(owner_token + 1)
    slice_width = FF // N_TENSOR

    def expert_rows(index):
        entries = table[index]
        gathered = tokens[jnp.maximum(entries - 1, 0)]
        rows_in = jnp.where((entries > 0)[:, None], gathered, jnp.zeros_like(gathered))
        upward = jnp.dot(rows_in, w_up[index], preferred_element_type=jnp.float32)
        hidden = jax.nn.silu(upward).astype(jnp.bfloat16)
        split_hidden = hidden.reshape(-1, N_TENSOR, slice_width).astype(jnp.float32)
        split_down = w_down[index].reshape(N_TENSOR, slice_width, D).astype(jnp.float32)
        terms = jnp.einsum("rtf,tfd->trd", split_hidden, split_down)
        rounded = lax.optimization_barrier(terms.astype(jnp.bfloat16))
        return jnp.sum(rounded.astype(jnp.float32), axis=0)

    partial_sums = lax.map(expert_rows, jnp.arange(EXPERTS, dtype=jnp.int32))
    picked = partial_sums[expert_ids, position].reshape(TOKENS, TOP, D)
    return jnp.sum(picked * gates[:, :, None], axis=1).astype(jnp.bfloat16)
```

```python
import jax
import jax.numpy as jnp
from jax import lax
from jax.sharding import PartitionSpec as P


def body(tokens, route_ids, gates, w_up, w_down):
    experts = lax.axis_size("expert")
    ids = jnp.arange(experts, dtype=jnp.int32)
    dense = jnp.sum(
        jnp.where(route_ids[:, :, None] == ids, gates[:, :, None], 0.0), axis=1
    )
    mine = lax.all_to_all(dense.T, "expert", split_axis=0, concat_axis=0, tiled=True).reshape(-1, 1)
    rows = lax.all_gather(tokens, "expert", axis=0, tiled=True)
    rows = lax.all_gather(rows, "tensor", axis=1, tiled=True)
    upward = jnp.dot(rows, w_up[0], preferred_element_type=jnp.float32)
    hidden = jax.nn.silu(upward).astype(jnp.bfloat16)
    out = jnp.dot(hidden, w_down[0], preferred_element_type=jnp.float32) * mine
    half = lax.psum_scatter(out.astype(jnp.bfloat16), "tensor", scatter_dimension=1, tiled=True)
    return lax.psum_scatter(half, "expert", scatter_dimension=0, tiled=True)


def solution(mesh):
    return jax.shard_map(
        body,
        mesh=mesh,
        in_specs=(
            P(("group", "expert"), "tensor"),
            P(("group", "expert"), None),
            P(("group", "expert"), None),
            P("expert", None, "tensor"),
            P("expert", "tensor", None),
        ),
        out_specs=P(("group", "expert"), "tensor"),
        check_vma=False,
    )
```

```python
import jax
import jax.numpy as jnp
from jax import lax
from jax.experimental import pallas as pl
from jax.experimental.pallas import tpu as pltpu
from jax.sharding import PartitionSpec as P

F32, BF16 = jnp.float32, jnp.bfloat16
TILE = 512


def layer_kernel(
    tok, ids, gts, wu_hbm, wd_hbm, out,
    wu, wd, X, H, GS, GR, GB, DS, DR, A, XS, XR, R, CS, CU,
    wu_sem, wd_sem, zs, zr, xs, xr, ds, dr, gs, gr, ds2, dr2, xs2, xr2, chs, chr_,
):
    rows, half = tok.shape
    ff = wu.shape[1]
    pieces = half // TILE
    e, t = lax.axis_index("expert"), lax.axis_index("tensor")
    z, x = e // 2, e % 2
    sib, partner = 1 - t, 2 * z + 1 - x
    interior = (z % 3) > 0
    end = (z % 3) == 0
    order = [z, 1 + z % 2, (2 + 3 * z) % 5, 3 * (1 - z // 2)]

    def remote(src, dst, ss, rs, **dev):
        return pltpu.make_async_remote_copy(
            src, dst, ss, rs, device_id=dev, device_id_type=pl.DeviceIdType.MESH
        )

    def mult(v, m):
        return pl.multiple_of(v, m)

    def block(b):
        return X.at[t, pl.ds(mult(b * rows, rows), rows), :]

    starts = list(range(0, ff, TILE))

    def up_load(j):
        w = min(TILE, ff - starts[j])
        cols = pl.ds(starts[j], w)
        return pltpu.make_async_copy(wu_hbm.at[0, :, cols], wu.at[:, cols], wu_sem.at[j])

    def down_cols(p, own):
        h = t if own else sib
        return pl.ds(mult(h * half + p * TILE, TILE), TILE)

    def down_load(p, own):
        cols = down_cols(p, own)
        return pltpu.make_async_copy(wd_hbm.at[0, :, cols], wd.at[:, cols], wd_sem.at[p, own])

    for j in range(len(starts)):
        up_load(j).start()
    for p in range(pieces):
        down_load(p, 0).start()
        down_load(p, 1).start()

    barrier = pltpu.get_barrier_semaphore()
    for k in range(1, 8):
        pl.semaphore_signal(
            barrier, inc=1, device_id={"expert": (e + k) % 8}, device_id_type=pl.DeviceIdType.MESH
        )
    pl.semaphore_signal(barrier, inc=1, device_id={"tensor": sib}, device_id_type=pl.DeviceIdType.MESH)
    pl.semaphore_wait(barrier, 8)

    def z_send(s):
        return remote(tok, block(e), zs.at[s], zr.at[z], expert=order[s] * 2 + x)

    def z_recv(s):
        return remote(tok, block(order[s] * 2 + x), zs.at[s], zr.at[order[s]], expert=e)

    def x_copy(s):
        b = order[s] * 2 + x
        return remote(tok if s == 0 else block(b), block(b), xs.at[s], xr.at[s], expert=partner)

    def d_copy(s, j):
        b = order[s] * 2 + (x if j == 0 else 1 - x)
        src = tok if s == 0 and j == 0 else block(b)
        return remote(src, block(b), ds.at[s, j], dr.at[s, j], tensor=sib)

    def forward_a(s):
        if s:
            z_recv(s).wait_recv()
        x_copy(s).start()
        d_copy(s, 0).start()

    def forward_b(s):
        x_copy(s).wait_recv()
        d_copy(s, 1).start()

    def forward_c(s):
        d_copy(s, 0).wait_recv()
        d_copy(s, 1).wait_recv()

    forward_a(0)
    for s in (1, 2, 3):
        z_send(s).start()
    X[t, pl.ds(mult(e * rows, rows), rows), :] = tok[...]

    lane = lax.broadcasted_iota(jnp.int32, (rows, 128), 1)
    dense = jnp.zeros((rows, 128), F32)
    for k in range(ids.shape[1]):
        dense = dense + jnp.where(ids[:, k : k + 1] == lane, gts[:, k : k + 1], 0.0)
    dense = jnp.concatenate([dense, jnp.zeros((128 - rows, 128), F32)], axis=0)
    GS[...] = dense.T[0:8, :]
    GR[e] = GS[...]

    def g_copy(k):
        return remote(GS, GR.at[e], gs.at[k], gr.at[e], expert=(e + k) % 8)

    def g_recv(k):
        o = (e + k) % 8
        return remote(GS, GR.at[o], gs.at[k], gr.at[o], expert=o)

    for k in range(1, 8):
        g_copy(k).start()
    forward_a(1)
    for k in range(1, 8):
        g_recv(k).wait_recv()
    mine = lax.broadcasted_iota(jnp.int32, (8, 128), 0) == e

    @pl.loop(0, 8)
    def _(b):
        row = jnp.sum(jnp.where(mine, GR[b], 0.0), axis=0, keepdims=True)
        full = jnp.broadcast_to(row, (128, 128)).T
        GB[pl.ds(mult(b * rows, rows), rows), :] = full[0:rows, :]

    def up(s):
        rs = pl.ds(mult(order[s] * 2 * rows, 2 * rows), 2 * rows)

        def tile(cols):
            v = jnp.dot(X[0, rs, :], wu[0:half, cols], preferred_element_type=F32)
            v = v + jnp.dot(X[1, rs, :], wu[half : 2 * half, cols], preferred_element_type=F32)
            H[:, cols] = (v / (1.0 + jnp.exp(-v))).astype(BF16)

        full = ff // TILE
        if s == 0:
            @pl.loop(0, full)
            def _(j):
                cols = pl.ds(mult(j * TILE, TILE), TILE)
                pltpu.make_async_copy(wu_hbm.at[0, :, cols], wu.at[:, cols], wu_sem.at[j]).wait()
                tile(cols)
        else:
            @pl.loop(0, full)
            def _(j):
                tile(pl.ds(mult(j * TILE, TILE), TILE))
        if ff % TILE:
            if s == 0:
                up_load(full).wait()
            tile(pl.ds(full * TILE, ff % TILE))

    def d2(q):
        return remote(DS.at[q], DR.at[q], ds2.at[q], dr2.at[q], tensor=sib)

    def x2(q):
        return remote(XS.at[q], XR.at[q], xs2.at[q], xr2.at[q], expert=partner)

    def chain(q, c, u, p):
        return remote(CS.at[q], CU.at[u, c, p], chs.at[q], chr_.at[u, c, p], expert=e + 4 * u - 2)

    mine_rows = pl.ds(mult(x * rows, rows), rows)
    other_rows = pl.ds(mult((1 - x) * rows, rows), rows)

    def stage_b(q):
        d2(q).wait_recv()
        XS[q] = (A[q, other_rows, :] + DR[q, other_rows, :].astype(F32)).astype(BF16)
        x2(q).start()
        R[q] = A[q, mine_rows, :] + DR[q, mine_rows, :].astype(F32)

    def stage_c(q):
        x2(q).wait_recv()
        r = R[q] + XR[q].astype(F32)
        R[q] = r
        s, p = q // pieces, q % pieces

        @pl.when(end & (q >= pieces))
        def _():
            CS[q] = r.astype(BF16)
            chain(q, z + s * (1 - 2 * (z // 3)), 1 - z // 3, p).start()

    def down(s):
        rs = pl.ds(mult(order[s] * 2 * rows, 2 * rows), 2 * rows)

        @pl.loop(0, pieces)
        def _(p):
            q = s * pieces + p
            gate = jnp.concatenate([GB[rs, :]] * (TILE // 128), axis=1)
            if s == 0:
                down_load(p, 0).wait()
            v = jnp.dot(H[...], wd[:, down_cols(p, 0)], preferred_element_type=F32)
            DS[q] = (v * gate).astype(BF16)
            d2(q).start()
            if s == 0:
                down_load(p, 1).wait()
            v = jnp.dot(H[...], wd[:, down_cols(p, 1)], preferred_element_type=F32)
            A[q] = v * gate
            pl.when(q >= 1)(lambda: stage_b(q - 1))
            pl.when(q >= 2)(lambda: stage_c(q - 2))

    forward_b(0)
    forward_c(0)
    for s in range(4):
        up(s)
        if s + 2 < 4:
            forward_a(s + 2)
        if s + 1 < 4:
            forward_b(s + 1)
        down(s)
        if s + 1 < 4:
            forward_c(s + 1)
    last = 4 * pieces - 1
    stage_b(last)
    stage_c(last - 1)
    stage_c(last)

    @pl.when(interior)
    def _():
        for s in (1, 3, 2):
            c, u = order[s], (1 - z % 2) if s == 2 else (1 - z // 2)

            @pl.loop(0, pieces)
            def _(p):
                q = s * pieces + p
                remote(CS.at[q], CU.at[u, c, p], chs.at[q], chr_.at[u, c, p], expert=e).wait_recv()
                CS[q] = (R[q] + CU[u, c, p].astype(F32)).astype(BF16)
                chain(q, c, u, p).start()

    for p in range(pieces):
        for u, there in ((1, z > 0), (0, z < 3)):
            @pl.when(there)
            def _():
                remote(CS.at[p], CU.at[u, z, p], chs.at[p], chr_.at[u, z, p], expert=e).wait_recv()
                R[p] += CU[u, z, p].astype(F32)
        out[:, p * TILE : (p + 1) * TILE] = R[p].astype(BF16)

    for s in range(4):
        if s:
            z_send(s).wait_send()
        x_copy(s).wait_send()
        d_copy(s, 0).wait_send()
        d_copy(s, 1).wait_send()
    for k in range(1, 8):
        g_copy(k).wait_send()

    @pl.loop(0, 4 * pieces)
    def _(q):
        d2(q).wait_send()
        x2(q).wait_send()

    @pl.loop(pieces, 4 * pieces)
    def _(q):
        remote(CS.at[q], CU.at[0, 0, 0], chs.at[q], chr_.at[0, 0, 0], expert=e).wait_send()


def fused(tokens, route_ids, gates, w_up, w_down):
    rows, half = tokens.shape
    d, ff = w_up.shape[1:]
    pieces = half // TILE
    q = 4 * pieces
    dma = pltpu.SemaphoreType.DMA
    vmem = pl.BlockSpec(memory_space=pltpu.VMEM)
    hbm = pl.BlockSpec(memory_space=pl.ANY)
    return pl.pallas_call(
        layer_kernel,
        out_shape=jax.ShapeDtypeStruct((rows, half), BF16),
        in_specs=[vmem, vmem, vmem, hbm, hbm],
        out_specs=vmem,
        scratch_shapes=[
            pltpu.VMEM((d, ff), BF16),
            pltpu.VMEM((ff, d), BF16),
            pltpu.VMEM((2, 8 * rows, half), BF16),
            pltpu.VMEM((2 * rows, ff), BF16),
            pltpu.VMEM((8, 128), F32),
            pltpu.VMEM((8, 8, 128), F32),
            pltpu.VMEM((8 * rows, 128), F32),
            pltpu.VMEM((q, 2 * rows, TILE), BF16),
            pltpu.VMEM((q, 2 * rows, TILE), BF16),
            pltpu.VMEM((q, 2 * rows, TILE), F32),
            pltpu.VMEM((q, rows, TILE), BF16),
            pltpu.VMEM((q, rows, TILE), BF16),
            pltpu.VMEM((q, rows, TILE), F32),
            pltpu.VMEM((q, rows, TILE), BF16),
            pltpu.VMEM((2, 4, pieces, rows, TILE), BF16),
            dma((pl.cdiv(ff, TILE),)),
            dma((pieces, 2)),
            dma((4,)), dma((4,)), dma((4,)), dma((4,)),
            dma((4, 2)), dma((4, 2)),
            dma((8,)), dma((8,)),
            dma((q,)), dma((q,)), dma((q,)), dma((q,)),
            dma((q,)), dma((2, 4, pieces)),
        ],
        compiler_params=pltpu.CompilerParams(
            collective_id=0, has_side_effects=True, vmem_limit_bytes=60 * 2**20
        ),
    )(tokens, route_ids, gates, w_up, w_down)


def general(tokens, route_ids, gates, w_up, w_down):
    experts = lax.axis_size("expert")
    tok_rows, per_token = route_ids.shape
    capacity = min(tok_rows, 2 * tok_rows * per_token // experts)
    flat_ids = route_ids.reshape(-1)
    onehot = (flat_ids[:, None] == jnp.arange(experts, dtype=jnp.int32)[None, :]).astype(jnp.int32)
    within = jnp.sum((jnp.cumsum(onehot, axis=0) - onehot) * onehot, axis=1)
    target = flat_ids * capacity + within
    slots = jnp.zeros((experts * capacity, tokens.shape[1]), tokens.dtype)
    slots = slots.at[target].set(jnp.repeat(tokens, per_token, axis=0))
    arrived = lax.all_to_all(slots, "expert", split_axis=0, concat_axis=0, tiled=True)
    arrived = lax.all_gather(arrived, "tensor", axis=1, tiled=True)
    upward = jnp.dot(arrived, w_up[0], preferred_element_type=F32)
    hidden = jax.nn.silu(upward).astype(BF16)
    partial = jnp.dot(hidden, w_down[0], preferred_element_type=F32).astype(BF16)
    results = lax.psum_scatter(partial, "tensor", scatter_dimension=1, tiled=True)
    returned = lax.all_to_all(results, "expert", split_axis=0, concat_axis=0, tiled=True)
    picked = returned[target].reshape(tok_rows, per_token, -1).astype(F32)
    return jnp.sum(picked * gates[:, :, None], axis=1).astype(BF16)


def solution(mesh):
    def body(tokens, route_ids, gates, w_up, w_down):
        rows, half = tokens.shape
        fits = mesh.shape["expert"] == 8 and mesh.shape["tensor"] == 2
        fits = fits and rows == 64 and half % TILE == 0 and w_up.shape[2] % 128 == 0
        form = fused if fits else general
        return form(tokens, route_ids, gates, w_up, w_down)

    return jax.shard_map(
        body,
        mesh=mesh,
        in_specs=(
            P(("group", "expert"), "tensor"),
            P(("group", "expert"), None),
            P(("group", "expert"), None),
            P("expert", None, "tensor"),
            P("expert", "tensor", None),
        ),
        out_specs=P(("group", "expert"), "tensor"),
        check_vma=False,
    )
```

```python
import jax
import jax.numpy as jnp
from jax import lax
from jax.experimental import pallas as pl
from jax.experimental.pallas import tpu as pltpu
from jax.sharding import PartitionSpec as P

F32, BF16 = jnp.float32, jnp.bfloat16
TILE = 512


def layer_kernel(
    tok, ids, gts, wu_hbm, wd_hbm, out,
    wu, wd, X, H, GS, GR, GB, DS, DR, A, XS, XR, R, CS, CU,
    wu_sem, wd_sem, zs, zr, xs, xr, ds, dr, gs, gr, ds2, dr2, xs2, xr2, chs, chr_,
):
    rows, half = tok.shape
    ff = wu.shape[1]
    pieces = half // TILE
    e, t = lax.axis_index("expert"), lax.axis_index("tensor")
    z, x = e // 2, e % 2
    sib, partner = 1 - t, 2 * z + 1 - x
    interior = (z % 3) > 0
    end = (z % 3) == 0
    pairs = [z // 2, 1 - z // 2]

    def remote(src, dst, ss, rs, **dev):
        return pltpu.make_async_remote_copy(
            src, dst, ss, rs, device_id=dev, device_id_type=pl.DeviceIdType.MESH
        )

    def mult(v, m):
        return pl.multiple_of(v, m)

    def block(b):
        return X.at[t, pl.ds(mult(b * rows, rows), rows), :]

    starts = list(range(0, ff, TILE))

    def up_load(j):
        w = min(TILE, ff - starts[j])
        cols = pl.ds(starts[j], w)
        return pltpu.make_async_copy(wu_hbm.at[0, :, cols], wu.at[:, cols], wu_sem.at[j])

    def down_cols(p, own):
        h = t if own else sib
        return pl.ds(mult(h * half + p * TILE, TILE), TILE)

    def down_load(p, own):
        cols = down_cols(p, own)
        return pltpu.make_async_copy(wd_hbm.at[0, :, cols], wd.at[:, cols], wd_sem.at[p, own])

    for j in range(len(starts)):
        up_load(j).start()
    for p in range(pieces):
        down_load(p, 0).start()
        down_load(p, 1).start()

    barrier = pltpu.get_barrier_semaphore()
    for k in range(1, 8):
        pl.semaphore_signal(
            barrier, inc=1, device_id={"expert": (e + k) % 8}, device_id_type=pl.DeviceIdType.MESH
        )
    pl.semaphore_signal(barrier, inc=1, device_id={"tensor": sib}, device_id_type=pl.DeviceIdType.MESH)
    pl.semaphore_wait(barrier, 8)

    def z_copy(c, up):
        src = block(c * 2 + x)
        return remote(src, src, zs.at[c, up], zr.at[c], expert=e + 4 * up - 2)

    def x_copy(c, src=None):
        b = block(c * 2 + x)
        return remote(b if src is None else src, b, xs.at[c], xr.at[c], expert=partner)

    def x_recv(c):
        x_copy(c).wait_recv()

    def d_copy(c, j, src=None):
        b = block(c * 2 + (x if j == 0 else 1 - x))
        return remote(b if src is None else src, b, ds.at[c, j], dr.at[c, j], tensor=sib)

    def own_send(up):
        return remote(tok, block(e), zs.at[z, up], zr.at[z], expert=e + 4 * up - 2)

    def arrive(h):
        for up in (1, 0):
            c = z - h if up else z + h

            @pl.when((c >= 0) if up else (c <= 3))
            def _():
                z_copy(c, up).wait_recv()
                pl.when((z < 3) if up else (z > 0))(lambda: z_copy(c, up).start())
                x_copy(c).start()
                d_copy(c, 0).start()

    def crossed(c):
        x_recv(c)
        d_copy(c, 1).start()

    def ready(c):
        d_copy(c, 0).wait_recv()
        d_copy(c, 1).wait_recv()

    pl.when(z < 3)(lambda: own_send(1).start())
    pl.when(z > 0)(lambda: own_send(0).start())
    x_copy(z, tok).start()
    d_copy(z, 0, tok).start()
    X[t, pl.ds(mult(e * rows, rows), rows), :] = tok[...]

    lane = lax.broadcasted_iota(jnp.int32, (rows, 128), 1)
    dense = jnp.zeros((rows, 128), F32)
    for k in range(ids.shape[1]):
        dense = dense + jnp.where(ids[:, k : k + 1] == lane, gts[:, k : k + 1], 0.0)
    dense = jnp.concatenate([dense, jnp.zeros((128 - rows, 128), F32)], axis=0)
    GS[...] = dense.T[0:8, :]
    GR[e] = GS[...]

    def g_copy(k):
        return remote(GS, GR.at[e], gs.at[k], gr.at[e], expert=(e + k) % 8)

    def g_recv(k):
        o = (e + k) % 8
        return remote(GS, GR.at[o], gs.at[k], gr.at[o], expert=o)

    for k in range(1, 8):
        g_copy(k).start()
    arrive(1)
    crossed(z)
    for k in range(1, 8):
        g_recv(k).wait_recv()
    mine = lax.broadcasted_iota(jnp.int32, (8, 128), 0) == e

    @pl.loop(0, 8)
    def _(b):
        row = jnp.sum(jnp.where(mine, GR[b], 0.0), axis=0, keepdims=True)
        full = jnp.broadcast_to(row, (128, 128)).T
        GB[pl.ds(mult(b * rows, rows), rows), :] = full[0:rows, :]

    def up(s):
        rs = pl.ds(mult(pairs[s] * 4 * rows, 4 * rows), 4 * rows)

        def tile(cols):
            v = jnp.dot(X[0, rs, :], wu[0:half, cols], preferred_element_type=F32)
            v = v + jnp.dot(X[1, rs, :], wu[half : 2 * half, cols], preferred_element_type=F32)
            H[:, cols] = (v / (1.0 + jnp.exp(-v))).astype(BF16)

        full = ff // TILE
        if s == 0:
            @pl.loop(0, full)
            def _(j):
                cols = pl.ds(mult(j * TILE, TILE), TILE)
                pltpu.make_async_copy(wu_hbm.at[0, :, cols], wu.at[:, cols], wu_sem.at[j]).wait()
                tile(cols)
        else:
            @pl.loop(0, full)
            def _(j):
                tile(pl.ds(mult(j * TILE, TILE), TILE))
        if ff % TILE:
            if s == 0:
                up_load(full).wait()
            tile(pl.ds(full * TILE, ff % TILE))

    def d2(q):
        return remote(DS.at[q], DR.at[q], ds2.at[q], dr2.at[q], tensor=sib)

    def x2(q):
        return remote(XS.at[q], XR.at[q], xs2.at[q], xr2.at[q], expert=partner)

    def chain(q, i, c, u, p):
        return remote(
            CS.at[q, i], CU.at[u, c, p], chs.at[q, i], chr_.at[u, c, p], expert=e + 4 * u - 2
        )

    def part(i, of):
        return pl.ds(mult((2 * i + of) * rows, rows), rows)

    def stage_b(q):
        d2(q).wait_recv()
        for i in range(2):
            rs = part(i, 1 - x)
            XS[q, i] = (A[q, rs, :] + DR[q, rs, :].astype(F32)).astype(BF16)
        x2(q).start()
        for i in range(2):
            rs = part(i, x)
            R[q, i] = A[q, rs, :] + DR[q, rs, :].astype(F32)

    def stage_c(q):
        x2(q).wait_recv()
        s, p = q // pieces, q % pieces
        for i in range(2):
            r = R[q, i] + XR[q, i].astype(F32)
            R[q, i] = r
            kind = (z + i) % 2 + 2 * s

            @pl.when(end & (kind >= 1))
            def _():
                CS[q, i] = r.astype(BF16)
                pair = z // 2 + s * (1 - 2 * (z // 2))
                chain(q, i, 2 * pair + i, 1 - z // 2, p).start()

    def down(s):
        rs = pl.ds(mult(pairs[s] * 4 * rows, 4 * rows), 4 * rows)

        @pl.loop(0, pieces)
        def _(p):
            q = s * pieces + p
            gate = jnp.concatenate([GB[rs, :]] * (TILE // 128), axis=1)
            if s == 0:
                down_load(p, 0).wait()
            v = jnp.dot(H[...], wd[:, down_cols(p, 0)], preferred_element_type=F32)
            DS[q] = (v * gate).astype(BF16)
            d2(q).start()
            if s == 0:
                down_load(p, 1).wait()
            v = jnp.dot(H[...], wd[:, down_cols(p, 1)], preferred_element_type=F32)
            A[q] = v * gate
            pl.when(q >= 1)(lambda: stage_b(q - 1))
            pl.when(q >= 2)(lambda: stage_c(q - 2))

    near = z + 1 - 2 * (z % 2)
    far = [pairs[1] * 2 + z // 2, pairs[1] * 2 + 1 - z // 2]
    arrive(2)
    crossed(near)
    ready(z)
    ready(near)
    up(0)
    arrive(3)
    crossed(far[0])
    down(0)
    crossed(far[1])
    ready(far[0])
    ready(far[1])
    up(1)
    down(1)
    last = 2 * pieces - 1
    stage_b(last)
    stage_c(last - 1)
    stage_c(last)

    def pass_on(q, i, c, u, p):
        remote(CS.at[q, i], CU.at[u, c, p], chs.at[q, i], chr_.at[u, c, p], expert=e).wait_recv()
        CS[q, i] = (R[q, i] + CU[u, c, p].astype(F32)).astype(BF16)
        chain(q, i, c, u, p).start()

    @pl.when(interior)
    def _():
        @pl.loop(0, pieces)
        def _(p):
            for k in (1, 0):
                pass_on(pieces + p, far[k] % 2, far[k], 1 - z // 2, p)

        @pl.loop(0, pieces)
        def _(p):
            pass_on(p, near % 2, near, z // 2, p)

    for p in range(pieces):
        for u, there in ((1, z > 0), (0, z < 3)):
            @pl.when(there)
            def _():
                remote(CS.at[p, 0], CU.at[u, z, p], chs.at[p, 0], chr_.at[u, z, p], expert=e).wait_recv()
                R[p, z % 2] += CU[u, z, p].astype(F32)
        out[:, p * TILE : (p + 1) * TILE] = R[p, z % 2].astype(BF16)

    pl.when(z < 3)(lambda: own_send(1).wait_send())
    pl.when(z > 0)(lambda: own_send(0).wait_send())
    for h in (1, 2, 3):
        pl.when((z - h >= 0) & (z < 3))(lambda: z_copy(z - h, 1).wait_send())
        pl.when((z + h <= 3) & (z > 0))(lambda: z_copy(z + h, 0).wait_send())
    for c in range(4):
        x_copy(c).wait_send()
        d_copy(c, 0).wait_send()
        d_copy(c, 1).wait_send()
    for k in range(1, 8):
        g_copy(k).wait_send()

    @pl.loop(0, 2 * pieces)
    def _(q):
        d2(q).wait_send()
        x2(q).wait_send()

    def sent(q, i):
        remote(CS.at[q, i], CU.at[0, 0, 0], chs.at[q, i], chr_.at[0, 0, 0], expert=e).wait_send()

    for p in range(pieces):
        sent(p, 1 - z % 2)
        sent(pieces + p, 0)
        sent(pieces + p, 1)


def fused(tokens, route_ids, gates, w_up, w_down):
    rows, half = tokens.shape
    d, ff = w_up.shape[1:]
    pieces = half // TILE
    q = 2 * pieces
    dma = pltpu.SemaphoreType.DMA
    vmem = pl.BlockSpec(memory_space=pltpu.VMEM)
    hbm = pl.BlockSpec(memory_space=pl.ANY)
    return pl.pallas_call(
        layer_kernel,
        out_shape=jax.ShapeDtypeStruct((rows, half), BF16),
        in_specs=[vmem, vmem, vmem, hbm, hbm],
        out_specs=vmem,
        scratch_shapes=[
            pltpu.VMEM((d, ff), BF16),
            pltpu.VMEM((ff, d), BF16),
            pltpu.VMEM((2, 8 * rows, half), BF16),
            pltpu.VMEM((4 * rows, ff), BF16),
            pltpu.VMEM((8, 128), F32),
            pltpu.VMEM((8, 8, 128), F32),
            pltpu.VMEM((8 * rows, 128), F32),
            pltpu.VMEM((q, 4 * rows, TILE), BF16),
            pltpu.VMEM((q, 4 * rows, TILE), BF16),
            pltpu.VMEM((q, 4 * rows, TILE), F32),
            pltpu.VMEM((q, 2, rows, TILE), BF16),
            pltpu.VMEM((q, 2, rows, TILE), BF16),
            pltpu.VMEM((q, 2, rows, TILE), F32),
            pltpu.VMEM((q, 2, rows, TILE), BF16),
            pltpu.VMEM((2, 4, pieces, rows, TILE), BF16),
            dma((pl.cdiv(ff, TILE),)),
            dma((pieces, 2)),
            dma((4, 2)), dma((4,)), dma((4,)), dma((4,)),
            dma((4, 2)), dma((4, 2)),
            dma((8,)), dma((8,)),
            dma((q,)), dma((q,)), dma((q,)), dma((q,)),
            dma((q, 2)), dma((2, 4, pieces)),
        ],
        compiler_params=pltpu.CompilerParams(
            collective_id=0, has_side_effects=True, vmem_limit_bytes=60 * 2**20
        ),
    )(tokens, route_ids, gates, w_up, w_down)


def general(tokens, route_ids, gates, w_up, w_down):
    experts = lax.axis_size("expert")
    tok_rows, per_token = route_ids.shape
    capacity = min(tok_rows, 2 * tok_rows * per_token // experts)
    flat_ids = route_ids.reshape(-1)
    onehot = (flat_ids[:, None] == jnp.arange(experts, dtype=jnp.int32)[None, :]).astype(jnp.int32)
    within = jnp.sum((jnp.cumsum(onehot, axis=0) - onehot) * onehot, axis=1)
    target = flat_ids * capacity + within
    slots = jnp.zeros((experts * capacity, tokens.shape[1]), tokens.dtype)
    slots = slots.at[target].set(jnp.repeat(tokens, per_token, axis=0))
    arrived = lax.all_to_all(slots, "expert", split_axis=0, concat_axis=0, tiled=True)
    arrived = lax.all_gather(arrived, "tensor", axis=1, tiled=True)
    upward = jnp.dot(arrived, w_up[0], preferred_element_type=F32)
    hidden = jax.nn.silu(upward).astype(BF16)
    partial = jnp.dot(hidden, w_down[0], preferred_element_type=F32).astype(BF16)
    results = lax.psum_scatter(partial, "tensor", scatter_dimension=1, tiled=True)
    returned = lax.all_to_all(results, "expert", split_axis=0, concat_axis=0, tiled=True)
    picked = returned[target].reshape(tok_rows, per_token, -1).astype(F32)
    return jnp.sum(picked * gates[:, :, None], axis=1).astype(BF16)


def solution(mesh):
    def body(tokens, route_ids, gates, w_up, w_down):
        rows, half = tokens.shape
        fits = mesh.shape["expert"] == 8 and mesh.shape["tensor"] == 2
        fits = fits and rows == 64 and half % TILE == 0 and w_up.shape[2] % 128 == 0
        form = fused if fits else general
        return form(tokens, route_ids, gates, w_up, w_down)

    return jax.shard_map(
        body,
        mesh=mesh,
        in_specs=(
            P(("group", "expert"), "tensor"),
            P(("group", "expert"), None),
            P(("group", "expert"), None),
            P("expert", None, "tensor"),
            P("expert", "tensor", None),
        ),
        out_specs=P(("group", "expert"), "tensor"),
        check_vma=False,
    )
```

```python
import jax
import jax.numpy as jnp
from jax import lax
from jax.experimental import pallas as pl
from jax.experimental.pallas import tpu as pltpu
from jax.sharding import PartitionSpec as P

F32, BF16 = jnp.float32, jnp.bfloat16
TILE = 512


def layer_kernel(
    tok, ids, gts, wu_hbm, wd_hbm, out,
    wu, wd, X, H, GS, GR, GB, DS, DR, A, XS, XR, R, CS, CU,
    wu_sem, wd_sem, zs, zr, xs, xr, ds, dr, gs, gr, ds2, dr2, xs2, xr2, chs, chr_,
):
    rows, half = tok.shape
    ff = wu.shape[1]
    pieces = half // TILE
    e, t = lax.axis_index("expert"), lax.axis_index("tensor")
    z, x = e // 2, e % 2
    sib, partner = 1 - t, 2 * z + 1 - x
    interior = (z % 3) > 0
    end = (z % 3) == 0
    pairs = [z // 2, 1 - z // 2]

    def remote(src, dst, ss, rs, **dev):
        return pltpu.make_async_remote_copy(
            src, dst, ss, rs, device_id=dev, device_id_type=pl.DeviceIdType.MESH
        )

    def mult(v, m):
        return pl.multiple_of(v, m)

    def block(b):
        return X.at[t, pl.ds(mult(b * rows, rows), rows), :]

    starts = list(range(0, ff, TILE))

    def up_load(j):
        w = min(TILE, ff - starts[j])
        cols = pl.ds(starts[j], w)
        return pltpu.make_async_copy(wu_hbm.at[0, :, cols], wu.at[:, cols], wu_sem.at[j])

    def down_cols(p, own):
        h = t if own else sib
        return pl.ds(mult(h * half + p * TILE, TILE), TILE)

    def down_load(p, own):
        cols = down_cols(p, own)
        return pltpu.make_async_copy(wd_hbm.at[0, :, cols], wd.at[:, cols], wd_sem.at[p, own])

    for j in range(len(starts)):
        up_load(j).start()
    for p in range(pieces):
        down_load(p, 0).start()
        down_load(p, 1).start()

    barrier = pltpu.get_barrier_semaphore()
    for k in range(1, 8):
        pl.semaphore_signal(
            barrier, inc=1, device_id={"expert": (e + k) % 8}, device_id_type=pl.DeviceIdType.MESH
        )
    pl.semaphore_signal(barrier, inc=1, device_id={"tensor": sib}, device_id_type=pl.DeviceIdType.MESH)
    pl.semaphore_wait(barrier, 8)

    def z_copy(c, up):
        src = block(c * 2 + x)
        return remote(src, src, zs.at[c, up], zr.at[c], expert=e + 4 * up - 2)

    def x_copy(c, src=None):
        b = block(c * 2 + x)
        return remote(b if src is None else src, b, xs.at[c], xr.at[c], expert=partner)

    def x_recv(c):
        x_copy(c).wait_recv()

    def d_copy(c, j, src=None):
        b = block(c * 2 + (x if j == 0 else 1 - x))
        return remote(b if src is None else src, b, ds.at[c, j], dr.at[c, j], tensor=sib)

    def own_send(up):
        return remote(tok, block(e), zs.at[z, up], zr.at[z], expert=e + 4 * up - 2)

    def arrive(h):
        for up in (1, 0):
            c = z - h if up else z + h

            @pl.when((c >= 0) if up else (c <= 3))
            def _():
                z_copy(c, up).wait_recv()
                pl.when((z < 3) if up else (z > 0))(lambda: z_copy(c, up).start())
                x_copy(c).start()
                d_copy(c, 0).start()

    def crossed(c):
        x_recv(c)
        d_copy(c, 1).start()

    def ready(c):
        d_copy(c, 0).wait_recv()
        d_copy(c, 1).wait_recv()

    pl.when(z < 3)(lambda: own_send(1).start())
    pl.when(z > 0)(lambda: own_send(0).start())
    x_copy(z, tok).start()
    d_copy(z, 0, tok).start()
    X[t, pl.ds(mult(e * rows, rows), rows), :] = tok[...]

    expert_row = lax.broadcasted_iota(jnp.int32, (8, rows), 0)
    dense = jnp.zeros((8, rows), F32)
    for k in range(ids.shape[0]):
        dense = dense + jnp.where(ids[k : k + 1, :] == expert_row, gts[k : k + 1, :], 0.0)
    GS[...] = jnp.concatenate([dense, jnp.zeros((8, 128 - rows), F32)], axis=1)
    GR[e] = GS[...]

    def g_copy(k):
        return remote(GS, GR.at[e], gs.at[k], gr.at[e], expert=(e + k) % 8)

    def g_recv(k):
        o = (e + k) % 8
        return remote(GS, GR.at[o], gs.at[k], gr.at[o], expert=o)

    for k in range(1, 8):
        g_copy(k).start()
    arrive(1)
    crossed(z)
    for k in range(1, 8):
        g_recv(k).wait_recv()
    mine = lax.broadcasted_iota(jnp.int32, (8, 128), 0) == e

    @pl.loop(0, 8)
    def _(b):
        row = jnp.sum(jnp.where(mine, GR[b], 0.0), axis=0, keepdims=True)
        full = jnp.broadcast_to(row, (128, 128)).T
        GB[pl.ds(mult(b * rows, rows), rows), :] = full[0:rows, :]

    def up(s):
        rs = pl.ds(mult(pairs[s] * 4 * rows, 4 * rows), 4 * rows)

        def tile(cols):
            v = jnp.dot(X[0, rs, :], wu[0:half, cols], preferred_element_type=F32)
            v = v + jnp.dot(X[1, rs, :], wu[half : 2 * half, cols], preferred_element_type=F32)
            H[:, cols] = (v / (1.0 + jnp.exp(-v))).astype(BF16)

        full = ff // TILE
        if s == 0:
            @pl.loop(0, full)
            def _(j):
                cols = pl.ds(mult(j * TILE, TILE), TILE)
                pltpu.make_async_copy(wu_hbm.at[0, :, cols], wu.at[:, cols], wu_sem.at[j]).wait()
                tile(cols)
        else:
            @pl.loop(0, full)
            def _(j):
                tile(pl.ds(mult(j * TILE, TILE), TILE))
        if ff % TILE:
            if s == 0:
                up_load(full).wait()
            tile(pl.ds(full * TILE, ff % TILE))

    def d2(q):
        return remote(DS.at[q], DR.at[q], ds2.at[q], dr2.at[q], tensor=sib)

    def x2(q):
        return remote(XS.at[q], XR.at[q], xs2.at[q], xr2.at[q], expert=partner)

    def chain(q, i, c, u, p):
        return remote(
            CS.at[q, i], CU.at[u, c, p], chs.at[q, i], chr_.at[u, c, p], expert=e + 4 * u - 2
        )

    def part(i, of):
        return pl.ds(mult((2 * i + of) * rows, rows), rows)

    def stage_b(q):
        d2(q).wait_recv()
        for i in range(2):
            rs = part(i, 1 - x)
            XS[q, i] = (A[q, rs, :] + DR[q, rs, :].astype(F32)).astype(BF16)
        x2(q).start()
        for i in range(2):
            rs = part(i, x)
            R[q, i] = A[q, rs, :] + DR[q, rs, :].astype(F32)

    def stage_c(q):
        x2(q).wait_recv()
        s, p = q // pieces, q % pieces
        for i in range(2):
            r = R[q, i] + XR[q, i].astype(F32)
            R[q, i] = r
            kind = (z + i) % 2 + 2 * s

            @pl.when(end & (kind >= 1))
            def _():
                CS[q, i] = r.astype(BF16)
                pair = z // 2 + s * (1 - 2 * (z // 2))
                chain(q, i, 2 * pair + i, 1 - z // 2, p).start()

    def down(s):
        rs = pl.ds(mult(pairs[s] * 4 * rows, 4 * rows), 4 * rows)

        @pl.loop(0, pieces)
        def _(p):
            q = s * pieces + p
            gate = jnp.concatenate([GB[rs, :]] * (TILE // 128), axis=1)
            if s == 0:
                down_load(p, 0).wait()
            v = jnp.dot(H[...], wd[:, down_cols(p, 0)], preferred_element_type=F32)
            DS[q] = (v * gate).astype(BF16)
            d2(q).start()
            if s == 0:
                down_load(p, 1).wait()
            v = jnp.dot(H[...], wd[:, down_cols(p, 1)], preferred_element_type=F32)
            A[q] = v * gate
            pl.when(q >= 1)(lambda: stage_b(q - 1))
            pl.when(q >= 2)(lambda: stage_c(q - 2))

    near = z + 1 - 2 * (z % 2)
    far = [pairs[1] * 2 + z // 2, pairs[1] * 2 + 1 - z // 2]
    arrive(2)
    crossed(near)
    ready(z)
    ready(near)
    up(0)
    arrive(3)
    crossed(far[0])
    down(0)
    crossed(far[1])
    ready(far[0])
    ready(far[1])
    up(1)
    down(1)
    def pass_on(q, i, c, u, p):
        remote(CS.at[q, i], CU.at[u, c, p], chs.at[q, i], chr_.at[u, c, p], expert=e).wait_recv()
        CS[q, i] = (R[q, i] + CU[u, c, p].astype(F32)).astype(BF16)
        chain(q, i, c, u, p).start()

    def pass_far(p):
        @pl.when(interior)
        def _():
            for k in (1, 0):
                pass_on(pieces + p, far[k] % 2, far[k], 1 - z // 2, p)

    def pass_near(p):
        pl.when(interior)(lambda: pass_on(p, near % 2, near, z // 2, p))

    stage_b(2 * pieces - 1)
    for p in range(pieces):
        if p >= pieces - 2:
            stage_c(pieces + p)
        pass_far(p)
        if p:
            pass_near(p - 1)
    pass_near(pieces - 1)

    for p in range(pieces):
        for u, there in ((1, z > 0), (0, z < 3)):
            @pl.when(there)
            def _():
                remote(CS.at[p, 0], CU.at[u, z, p], chs.at[p, 0], chr_.at[u, z, p], expert=e).wait_recv()
                R[p, z % 2] += CU[u, z, p].astype(F32)
        out[:, p * TILE : (p + 1) * TILE] = R[p, z % 2].astype(BF16)

    pl.when(z < 3)(lambda: own_send(1).wait_send())
    pl.when(z > 0)(lambda: own_send(0).wait_send())
    for h in (1, 2, 3):
        pl.when((z - h >= 0) & (z < 3))(lambda: z_copy(z - h, 1).wait_send())
        pl.when((z + h <= 3) & (z > 0))(lambda: z_copy(z + h, 0).wait_send())
    for c in range(4):
        x_copy(c).wait_send()
        d_copy(c, 0).wait_send()
        d_copy(c, 1).wait_send()
    for k in range(1, 8):
        g_copy(k).wait_send()

    @pl.loop(0, 2 * pieces)
    def _(q):
        d2(q).wait_send()
        x2(q).wait_send()

    def sent(q, i):
        remote(CS.at[q, i], CU.at[0, 0, 0], chs.at[q, i], chr_.at[0, 0, 0], expert=e).wait_send()

    for p in range(pieces):
        sent(p, 1 - z % 2)
        sent(pieces + p, 0)
        sent(pieces + p, 1)


def fused(tokens, route_ids, gates, w_up, w_down):
    rows, half = tokens.shape
    d, ff = w_up.shape[1:]
    pieces = half // TILE
    q = 2 * pieces
    dma = pltpu.SemaphoreType.DMA
    vmem = pl.BlockSpec(memory_space=pltpu.VMEM)
    hbm = pl.BlockSpec(memory_space=pl.ANY)
    return pl.pallas_call(
        layer_kernel,
        out_shape=jax.ShapeDtypeStruct((rows, half), BF16),
        in_specs=[vmem, vmem, vmem, hbm, hbm],
        out_specs=vmem,
        scratch_shapes=[
            pltpu.VMEM((d, ff), BF16),
            pltpu.VMEM((ff, d), BF16),
            pltpu.VMEM((2, 8 * rows, half), BF16),
            pltpu.VMEM((4 * rows, ff), BF16),
            pltpu.VMEM((8, 128), F32),
            pltpu.VMEM((8, 8, 128), F32),
            pltpu.VMEM((8 * rows, 128), F32),
            pltpu.VMEM((q, 4 * rows, TILE), BF16),
            pltpu.VMEM((q, 4 * rows, TILE), BF16),
            pltpu.VMEM((q, 4 * rows, TILE), F32),
            pltpu.VMEM((q, 2, rows, TILE), BF16),
            pltpu.VMEM((q, 2, rows, TILE), BF16),
            pltpu.VMEM((q, 2, rows, TILE), F32),
            pltpu.VMEM((q, 2, rows, TILE), BF16),
            pltpu.VMEM((2, 4, pieces, rows, TILE), BF16),
            dma((pl.cdiv(ff, TILE),)),
            dma((pieces, 2)),
            dma((4, 2)), dma((4,)), dma((4,)), dma((4,)),
            dma((4, 2)), dma((4, 2)),
            dma((8,)), dma((8,)),
            dma((q,)), dma((q,)), dma((q,)), dma((q,)),
            dma((q, 2)), dma((2, 4, pieces)),
        ],
        compiler_params=pltpu.CompilerParams(
            collective_id=0, has_side_effects=True, vmem_limit_bytes=60 * 2**20
        ),
    )(tokens, route_ids.T, gates.T, w_up, w_down)


def general(tokens, route_ids, gates, w_up, w_down):
    experts = lax.axis_size("expert")
    tok_rows, per_token = route_ids.shape
    capacity = min(tok_rows, 2 * tok_rows * per_token // experts)
    flat_ids = route_ids.reshape(-1)
    onehot = (flat_ids[:, None] == jnp.arange(experts, dtype=jnp.int32)[None, :]).astype(jnp.int32)
    within = jnp.sum((jnp.cumsum(onehot, axis=0) - onehot) * onehot, axis=1)
    target = flat_ids * capacity + within
    slots = jnp.zeros((experts * capacity, tokens.shape[1]), tokens.dtype)
    slots = slots.at[target].set(jnp.repeat(tokens, per_token, axis=0))
    arrived = lax.all_to_all(slots, "expert", split_axis=0, concat_axis=0, tiled=True)
    arrived = lax.all_gather(arrived, "tensor", axis=1, tiled=True)
    upward = jnp.dot(arrived, w_up[0], preferred_element_type=F32)
    hidden = jax.nn.silu(upward).astype(BF16)
    partial = jnp.dot(hidden, w_down[0], preferred_element_type=F32).astype(BF16)
    results = lax.psum_scatter(partial, "tensor", scatter_dimension=1, tiled=True)
    returned = lax.all_to_all(results, "expert", split_axis=0, concat_axis=0, tiled=True)
    picked = returned[target].reshape(tok_rows, per_token, -1).astype(F32)
    return jnp.sum(picked * gates[:, :, None], axis=1).astype(BF16)


def solution(mesh):
    def body(tokens, route_ids, gates, w_up, w_down):
        rows, half = tokens.shape
        fits = mesh.shape["expert"] == 8 and mesh.shape["tensor"] == 2
        fits = fits and rows == 64 and half % TILE == 0 and w_up.shape[2] % 128 == 0
        form = fused if fits else general
        return form(tokens, route_ids, gates, w_up, w_down)

    return jax.shard_map(
        body,
        mesh=mesh,
        in_specs=(
            P(("group", "expert"), "tensor"),
            P(("group", "expert"), None),
            P(("group", "expert"), None),
            P("expert", None, "tensor"),
            P("expert", "tensor", None),
        ),
        out_specs=P(("group", "expert"), "tensor"),
        check_vma=False,
    )
```

```python
import jax
import jax.numpy as jnp
from jax import lax
from jax.experimental import pallas as pl
from jax.experimental.pallas import tpu as pltpu
from jax.sharding import PartitionSpec as P

F32, BF16 = jnp.float32, jnp.bfloat16
TILE = 512


def layer_kernel(
    tok, ids, gts, wu_hbm, wd_hbm, out,
    wu, wd, X, H, GS, GR, GB, DS, DR, A, XS, XR, R, CS, CU,
    wu_sem, wd_sem, zs, zr, xs, xr, ds, dr, gs, gr, ds2, dr2, xs2, xr2, chs, chr_,
):
    rows, half = tok.shape
    ff = wu.shape[1]
    pieces = half // TILE
    e, t = lax.axis_index("expert"), lax.axis_index("tensor")
    z, x = e // 2, e % 2
    sib, partner = 1 - t, 2 * z + 1 - x
    interior = (z % 3) > 0
    end = (z % 3) == 0
    pairs = [z // 2, 1 - z // 2]

    def remote(src, dst, ss, rs, **dev):
        return pltpu.make_async_remote_copy(
            src, dst, ss, rs, device_id=dev, device_id_type=pl.DeviceIdType.MESH
        )

    def mult(v, m):
        return pl.multiple_of(v, m)

    def block(b):
        return X.at[t, pl.ds(mult(b * rows, rows), rows), :]

    starts = list(range(0, ff, TILE))

    def up_load(j):
        w = min(TILE, ff - starts[j])
        cols = pl.ds(starts[j], w)
        return pltpu.make_async_copy(wu_hbm.at[0, :, cols], wu.at[:, cols], wu_sem.at[j])

    def down_cols(p, own):
        h = t if own else sib
        return pl.ds(mult(h * half + p * TILE, TILE), TILE)

    def down_load(p, own):
        cols = down_cols(p, own)
        return pltpu.make_async_copy(wd_hbm.at[0, :, cols], wd.at[:, cols], wd_sem.at[p, own])

    for j in range(len(starts)):
        up_load(j).start()
    for p in range(pieces):
        down_load(p, 0).start()
        down_load(p, 1).start()

    barrier = pltpu.get_barrier_semaphore()
    for k in range(1, 8):
        pl.semaphore_signal(
            barrier, inc=1, device_id={"expert": (e + k) % 8}, device_id_type=pl.DeviceIdType.MESH
        )
    pl.semaphore_signal(barrier, inc=1, device_id={"tensor": sib}, device_id_type=pl.DeviceIdType.MESH)
    pl.semaphore_wait(barrier, 8)

    def z_copy(c, up):
        src = block(c * 2 + x)
        return remote(src, src, zs.at[c, up], zr.at[c], expert=e + 4 * up - 2)

    def x_copy(c, src=None):
        b = block(c * 2 + x)
        return remote(b if src is None else src, b, xs.at[c], xr.at[c], expert=partner)

    def x_recv(c):
        x_copy(c).wait_recv()

    def d_copy(c, j, src=None):
        b = block(c * 2 + (x if j == 0 else 1 - x))
        return remote(b if src is None else src, b, ds.at[c, j], dr.at[c, j], tensor=sib)

    def own_send(up):
        return remote(tok, block(e), zs.at[z, up], zr.at[z], expert=e + 4 * up - 2)

    def arrive(h):
        for up in (1, 0):
            c = z - h if up else z + h

            @pl.when((c >= 0) if up else (c <= 3))
            def _():
                z_copy(c, up).wait_recv()
                pl.when((z < 3) if up else (z > 0))(lambda: z_copy(c, up).start())
                x_copy(c).start()
                d_copy(c, 0).start()

    def crossed(c):
        x_recv(c)
        d_copy(c, 1).start()

    def ready(c):
        d_copy(c, 0).wait_recv()
        d_copy(c, 1).wait_recv()

    pl.when(z < 3)(lambda: own_send(1).start())
    pl.when(z > 0)(lambda: own_send(0).start())
    x_copy(z, tok).start()
    d_copy(z, 0, tok).start()
    X[t, pl.ds(mult(e * rows, rows), rows), :] = tok[...]

    expert_row = lax.broadcasted_iota(jnp.int32, (8, rows), 0)
    dense = jnp.zeros((8, rows), F32)
    for k in range(ids.shape[0]):
        dense = dense + jnp.where(ids[k : k + 1, :] == expert_row, gts[k : k + 1, :], 0.0)
    GS[...] = jnp.concatenate([dense, jnp.zeros((8, 128 - rows), F32)], axis=1)
    GR[e] = GS[...]

    def g_copy(k):
        return remote(GS, GR.at[e], gs.at[k], gr.at[e], expert=(e + k) % 8)

    def g_recv(k):
        o = (e + k) % 8
        return remote(GS, GR.at[o], gs.at[k], gr.at[o], expert=o)

    for k in range(1, 8):
        g_copy(k).start()
    arrive(1)
    crossed(z)
    for k in range(1, 8):
        g_recv(k).wait_recv()
    mine = lax.broadcasted_iota(jnp.int32, (8, 128), 0) == e

    @pl.loop(0, 8)
    def _(b):
        row = jnp.sum(jnp.where(mine, GR[b], 0.0), axis=0, keepdims=True)
        full = jnp.broadcast_to(row, (128, 128)).T
        GB[pl.ds(mult(b * rows, rows), rows), :] = full[0:rows, :]

    def up(s):
        rs = pl.ds(mult(pairs[s] * 4 * rows, 4 * rows), 4 * rows)

        def tile(cols):
            v = jnp.dot(X[0, rs, :], wu[0:half, cols], preferred_element_type=F32)
            v = v + jnp.dot(X[1, rs, :], wu[half : 2 * half, cols], preferred_element_type=F32)
            H[:, cols] = (v / (1.0 + jnp.exp(-v))).astype(BF16)

        full = ff // TILE
        if s == 0:
            @pl.loop(0, full)
            def _(j):
                cols = pl.ds(mult(j * TILE, TILE), TILE)
                pltpu.make_async_copy(wu_hbm.at[0, :, cols], wu.at[:, cols], wu_sem.at[j]).wait()
                tile(cols)
        else:
            @pl.loop(0, full)
            def _(j):
                tile(pl.ds(mult(j * TILE, TILE), TILE))
        if ff % TILE:
            if s == 0:
                up_load(full).wait()
            tile(pl.ds(full * TILE, ff % TILE))

    def d2(q):
        return remote(DS.at[q], DR.at[q], ds2.at[q], dr2.at[q], tensor=sib)

    def x2(q):
        return remote(XS.at[q], XR.at[q], xs2.at[q], xr2.at[q], expert=partner)

    def chain(q, i, c, u, p):
        return remote(
            CS.at[q, i], CU.at[u, c, p], chs.at[q, i], chr_.at[u, c, p], expert=e + 4 * u - 2
        )

    def part(i, of):
        return pl.ds(mult((2 * i + of) * rows, rows), rows)

    def stage_b(q):
        d2(q).wait_recv()
        for i in range(2):
            rs = part(i, 1 - x)
            XS[q, i] = (A[q, rs, :] + DR[q, rs, :].astype(F32)).astype(BF16)
        x2(q).start()
        for i in range(2):
            rs = part(i, x)
            R[q, i] = A[q, rs, :] + DR[q, rs, :].astype(F32)

    def stage_c(q):
        x2(q).wait_recv()
        s, p = q // pieces, q % pieces
        for i in range(2):
            r = R[q, i] + XR[q, i].astype(F32)
            R[q, i] = r
            kind = (z + i) % 2 + 2 * s

            @pl.when(end & (kind >= 1))
            def _():
                CS[q, i] = r.astype(BF16)
                pair = z // 2 + s * (1 - 2 * (z // 2))
                chain(q, i, 2 * pair + i, 1 - z // 2, p).start()

    def down(s):
        rs = pl.ds(mult(pairs[s] * 4 * rows, 4 * rows), 4 * rows)

        @pl.loop(0, pieces)
        def _(p):
            q = s * pieces + p
            gate = jnp.concatenate([GB[rs, :]] * (TILE // 128), axis=1)
            if s == 0:
                down_load(p, 0).wait()
            v = jnp.dot(H[...], wd[:, down_cols(p, 0)], preferred_element_type=F32)
            DS[q] = (v * gate).astype(BF16)
            d2(q).start()
            if s == 0:
                down_load(p, 1).wait()
            v = jnp.dot(H[...], wd[:, down_cols(p, 1)], preferred_element_type=F32)
            A[q] = v * gate
            stage_b(q)
            pl.when(q >= 2)(lambda: stage_c(q - 2))

    near = z + 1 - 2 * (z % 2)
    far = [pairs[1] * 2 + z // 2, pairs[1] * 2 + 1 - z // 2]
    arrive(2)
    crossed(near)
    ready(z)
    ready(near)
    up(0)
    arrive(3)
    crossed(far[0])
    down(0)
    crossed(far[1])
    ready(far[0])
    ready(far[1])
    up(1)
    down(1)
    def pass_on(q, i, c, u, p):
        remote(CS.at[q, i], CU.at[u, c, p], chs.at[q, i], chr_.at[u, c, p], expert=e).wait_recv()
        CS[q, i] = (R[q, i] + CU[u, c, p].astype(F32)).astype(BF16)
        chain(q, i, c, u, p).start()

    def pass_far(p):
        @pl.when(interior)
        def _():
            for k in (1, 0):
                pass_on(pieces + p, far[k] % 2, far[k], 1 - z // 2, p)

    def pass_near(p):
        pl.when(interior)(lambda: pass_on(p, near % 2, near, z // 2, p))

    for p in range(pieces):
        if p >= pieces - 2:
            stage_c(pieces + p)
        pass_far(p)
        if p:
            pass_near(p - 1)
    pass_near(pieces - 1)

    for p in range(pieces):
        for u, there in ((1, z > 0), (0, z < 3)):
            @pl.when(there)
            def _():
                remote(CS.at[p, 0], CU.at[u, z, p], chs.at[p, 0], chr_.at[u, z, p], expert=e).wait_recv()
                R[p, z % 2] += CU[u, z, p].astype(F32)
        out[:, p * TILE : (p + 1) * TILE] = R[p, z % 2].astype(BF16)

    pl.when(z < 3)(lambda: own_send(1).wait_send())
    pl.when(z > 0)(lambda: own_send(0).wait_send())
    for h in (1, 2, 3):
        pl.when((z - h >= 0) & (z < 3))(lambda: z_copy(z - h, 1).wait_send())
        pl.when((z + h <= 3) & (z > 0))(lambda: z_copy(z + h, 0).wait_send())
    for c in range(4):
        x_copy(c).wait_send()
        d_copy(c, 0).wait_send()
        d_copy(c, 1).wait_send()
    for k in range(1, 8):
        g_copy(k).wait_send()

    @pl.loop(0, 2 * pieces)
    def _(q):
        d2(q).wait_send()
        x2(q).wait_send()

    def sent(q, i):
        remote(CS.at[q, i], CU.at[0, 0, 0], chs.at[q, i], chr_.at[0, 0, 0], expert=e).wait_send()

    for p in range(pieces):
        sent(p, 1 - z % 2)
        sent(pieces + p, 0)
        sent(pieces + p, 1)


def fused(tokens, route_ids, gates, w_up, w_down):
    rows, half = tokens.shape
    d, ff = w_up.shape[1:]
    pieces = half // TILE
    q = 2 * pieces
    dma = pltpu.SemaphoreType.DMA
    vmem = pl.BlockSpec(memory_space=pltpu.VMEM)
    hbm = pl.BlockSpec(memory_space=pl.ANY)
    return pl.pallas_call(
        layer_kernel,
        out_shape=jax.ShapeDtypeStruct((rows, half), BF16),
        in_specs=[vmem, vmem, vmem, hbm, hbm],
        out_specs=vmem,
        scratch_shapes=[
            pltpu.VMEM((d, ff), BF16),
            pltpu.VMEM((ff, d), BF16),
            pltpu.VMEM((2, 8 * rows, half), BF16),
            pltpu.VMEM((4 * rows, ff), BF16),
            pltpu.VMEM((8, 128), F32),
            pltpu.VMEM((8, 8, 128), F32),
            pltpu.VMEM((8 * rows, 128), F32),
            pltpu.VMEM((q, 4 * rows, TILE), BF16),
            pltpu.VMEM((q, 4 * rows, TILE), BF16),
            pltpu.VMEM((q, 4 * rows, TILE), F32),
            pltpu.VMEM((q, 2, rows, TILE), BF16),
            pltpu.VMEM((q, 2, rows, TILE), BF16),
            pltpu.VMEM((q, 2, rows, TILE), F32),
            pltpu.VMEM((q, 2, rows, TILE), BF16),
            pltpu.VMEM((2, 4, pieces, rows, TILE), BF16),
            dma((pl.cdiv(ff, TILE),)),
            dma((pieces, 2)),
            dma((4, 2)), dma((4,)), dma((4,)), dma((4,)),
            dma((4, 2)), dma((4, 2)),
            dma((8,)), dma((8,)),
            dma((q,)), dma((q,)), dma((q,)), dma((q,)),
            dma((q, 2)), dma((2, 4, pieces)),
        ],
        compiler_params=pltpu.CompilerParams(
            collective_id=0, has_side_effects=True, vmem_limit_bytes=60 * 2**20
        ),
    )(tokens, route_ids.T, gates.T, w_up, w_down)


def general(tokens, route_ids, gates, w_up, w_down):
    experts = lax.axis_size("expert")
    tok_rows, per_token = route_ids.shape
    capacity = min(tok_rows, 2 * tok_rows * per_token // experts)
    flat_ids = route_ids.reshape(-1)
    onehot = (flat_ids[:, None] == jnp.arange(experts, dtype=jnp.int32)[None, :]).astype(jnp.int32)
    within = jnp.sum((jnp.cumsum(onehot, axis=0) - onehot) * onehot, axis=1)
    target = flat_ids * capacity + within
    slots = jnp.zeros((experts * capacity, tokens.shape[1]), tokens.dtype)
    slots = slots.at[target].set(jnp.repeat(tokens, per_token, axis=0))
    arrived = lax.all_to_all(slots, "expert", split_axis=0, concat_axis=0, tiled=True)
    arrived = lax.all_gather(arrived, "tensor", axis=1, tiled=True)
    upward = jnp.dot(arrived, w_up[0], preferred_element_type=F32)
    hidden = jax.nn.silu(upward).astype(BF16)
    partial = jnp.dot(hidden, w_down[0], preferred_element_type=F32).astype(BF16)
    results = lax.psum_scatter(partial, "tensor", scatter_dimension=1, tiled=True)
    returned = lax.all_to_all(results, "expert", split_axis=0, concat_axis=0, tiled=True)
    picked = returned[target].reshape(tok_rows, per_token, -1).astype(F32)
    return jnp.sum(picked * gates[:, :, None], axis=1).astype(BF16)


def solution(mesh):
    def body(tokens, route_ids, gates, w_up, w_down):
        rows, half = tokens.shape
        fits = mesh.shape["expert"] == 8 and mesh.shape["tensor"] == 2
        fits = fits and rows == 64 and half % TILE == 0 and w_up.shape[2] % 128 == 0
        form = fused if fits else general
        return form(tokens, route_ids, gates, w_up, w_down)

    return jax.shard_map(
        body,
        mesh=mesh,
        in_specs=(
            P(("group", "expert"), "tensor"),
            P(("group", "expert"), None),
            P(("group", "expert"), None),
            P("expert", None, "tensor"),
            P("expert", "tensor", None),
        ),
        out_specs=P(("group", "expert"), "tensor"),
        check_vma=False,
    )
```
